32 devices in a mesh: ctx: 8 (over z, y), head: 4 (over x, core).
Axes of the slice: x: 2, y: 2, z: 4, core: 2. Of those that a mesh axis runs over, the one named last changes fastest.
Arguments:
- query: bfloat16 [4096, 4096], P(('ctx', 'head')), may hold values from -16 to 16
- key: bfloat16 [4096, 4096], P(('ctx', 'head')), may hold values from -4.5 to 4.5
- value: bfloat16 [4096, 4096], P(('ctx', 'head')), may hold values from -12 to 12
- out_grad: bfloat16 [4096, 4096], P(('ctx', 'head')), may hold values from -6 to 6
- offsets: int32 [2, 32], P(None, 'head'), may hold values from 0 to 63, as said below
Outputs:
- attended: bfloat16 [4096, 4096], P(('ctx', 'head'))
- query_grad: bfloat16 [4096, 4096], P(('ctx', 'head'))
- key_grad: bfloat16 [4096, 4096], P(('ctx', 'head'))
- value_grad: bfloat16 [4096, 4096], P(('ctx', 'head'))
The draws below stay inside these ranges and needn't reach their ends.
Inputs may be any that keep to these rules, and one draw needn't show every extreme that they name: `offsets`: row 0 holds values 0 to 15 with 15 among them; row 1 holds values 0 to 63 with 63 among them.
All inputs are finite; a program needn't handle non-finite values.
Results may differ from the reference program's by a relative error of at most 0.04.
Values may be sent and summed in bfloat16 or wider, within the bound.
A program may use at most 128 MiB of HBM per device.

```python
import jax
import jax.numpy as jnp
from jax import lax

HEADS = 32
HEAD_WIDTH = 128
TOKENS_PER_SLOT = 512
MIDDLE_DILATION = 16
UPPER_DILATION = 64
WIDTH = 4096
TOKEN_COUNT = 4096


def draw_key(key, part):
    key = jax.random.fold_in(key, 3)
    values = jnp.clip(jax.random.normal(key, (TOKEN_COUNT, HEADS * HEAD_WIDTH), jnp.float32), -4.0, 4.0)
    return values.astype(jnp.bfloat16)


def draw_query(key, part):
    key = jax.random.fold_in(key, 5)
    values = jnp.clip(jax.random.normal(jax.random.fold_in(key, 2), (TOKEN_COUNT, HEADS * HEAD_WIDTH), jnp.float32), -4.0, 4.0)
    return values.astype(jnp.bfloat16)


def draw_offsets(key, part):
    key = jax.random.fold_in(key, 11)
    raw = jax.random.randint(key, (2, HEADS), 0, 1 << 20)
    dilation_rates = jnp.array([MIDDLE_DILATION, UPPER_DILATION], jnp.int32)[:, None]
    values = raw % dilation_rates
    chosen = jax.random.randint(jax.random.fold_in(key, 1), (2, 1), 0, HEADS)
    columns = lax.broadcasted_iota(jnp.int32, (2, HEADS), 1)
    return jnp.where(columns == chosen, dilation_rates - 1, values).astype(jnp.int32)


def shard_levels(key, dims, cuts, low, high):
    loudness = 1.0
    for position, blocks in cuts:
        draws = jax.random.uniform(jax.random.fold_in(jax.random.fold_in(key, 6), position), (blocks,), jnp.float32, low / len(cuts), high / len(cuts))
        loudness = loudness * jnp.repeat(jnp.exp(draws), dims[position] // blocks).reshape((-1,) + (1,) * (len(dims) - 1 - position))
    return loudness


def gaussian(key, shape, width, most, cuts=(), held_as=jnp.bfloat16):
    entries = jax.random.normal(key, shape, jnp.float32) * width
    if len(cuts) > 0:
        entries = shard_levels(key, shape, cuts, -0.22, 0.18) * entries
    return jnp.clip(entries, min=-most, max=most).astype(held_as)


def setup_inputs(seed: int = 0) -> dict:
    key_list = jax.random.split(jax.random.key(seed), 6)
    query = draw_query(jax.random.fold_in(key_list[5], 71), 0)
    key = draw_key(jax.random.fold_in(key_list[5], 71), 0)
    value = gaussian(key_list[2], (TOKEN_COUNT, WIDTH), 3.0, 12.0, ((0, 32),))
    out_grad = gaussian(key_list[3], (TOKEN_COUNT, WIDTH), 1.0, 6.0, ((0, 32),))
    offsets = draw_offsets(jax.random.fold_in(key_list[5], 71), 0)
    return {"query": query, "key": key, "value": value, "out_grad": out_grad, "offsets": offsets}


def rounded_length(values):
    return lax.optimization_barrier(values.astype(jnp.bfloat16)).astype(jnp.float32)


def pick_rows(values, dilation_rate, start_offset):
    shaped = values.reshape((values.shape[0] // dilation_rate, dilation_rate) + values.shape[1:])
    return lax.dynamic_index_in_dim(shaped, start_offset, 1, keepdims=False)


def scatter_rows(full, rows, dilation_rate, start_offset, combine):
    shaped = full.reshape((full.shape[0] // dilation_rate, dilation_rate) + full.shape[1:])
    column = lax.dynamic_index_in_dim(shaped, start_offset, 1, keepdims=False)
    shaped = lax.dynamic_update_index_in_dim(shaped, combine(column, rows), start_offset, 1)
    return shaped.reshape(full.shape)


def one_head(items):
    query, key, value, grad, middle_offset, upper_offset = items
    softmax_scale = HEAD_WIDTH ** -0.5
    zero_offset = jnp.zeros((), jnp.int32)
    level_specifications = [(1, zero_offset, TOKEN_COUNT // TOKENS_PER_SLOT), (MIDDLE_DILATION, middle_offset.astype(jnp.int32), 4), (UPPER_DILATION, upper_offset.astype(jnp.int32), 1)]
    levels = []
    for dilation_rate, start_offset, segs in level_specifications:
        query_rows_local = pick_rows(query, dilation_rate, start_offset).reshape(segs, -1, HEAD_WIDTH).astype(jnp.float32)
        key_rows_local = pick_rows(key, dilation_rate, start_offset).reshape(segs, -1, HEAD_WIDTH).astype(jnp.float32)
        value_rows_local = pick_rows(value, dilation_rate, start_offset).reshape(segs, -1, HEAD_WIDTH).astype(jnp.float32)
        gradient_rows = pick_rows(grad, dilation_rate, start_offset).reshape(segs, -1, HEAD_WIDTH).astype(jnp.float32)
        logit_score = jnp.einsum('lrz,laz->lra', query_rows_local, key_rows_local) * softmax_scale
        levels.append((dilation_rate, start_offset, segs, query_rows_local, key_rows_local, value_rows_local, gradient_rows, logit_score))
    top = jnp.full((TOKEN_COUNT,), -jnp.inf, jnp.float32)
    for dilation_rate, start_offset, segs, query_rows_local, key_rows_local, value_rows_local, gradient_rows, logit_score in levels:
        top = scatter_rows(top, logit_score.max(-1).reshape(-1), dilation_rate, start_offset, jnp.maximum)
    total = jnp.zeros((TOKEN_COUNT,), jnp.float32)
    numer = jnp.zeros((TOKEN_COUNT, HEAD_WIDTH), jnp.float32)
    for dilation_rate, start_offset, segs, query_rows_local, key_rows_local, value_rows_local, gradient_rows, logit_score in levels:
        shift = pick_rows(top, dilation_rate, start_offset).reshape(segs, -1)
        level_weight = jnp.exp(logit_score - shift[..., None])
        total = scatter_rows(total, level_weight.sum(-1).reshape(-1), dilation_rate, start_offset, jnp.add)
        part = jnp.einsum('rtg,rgi->rti', rounded_length(level_weight), value_rows_local).reshape(-1, HEAD_WIDTH)
        numer = scatter_rows(numer, part, dilation_rate, start_offset, jnp.add)
    attended = (numer / total[:, None]).astype(jnp.bfloat16)
    lse = top + jnp.log(total)
    delta = jnp.sum(grad.astype(jnp.float32) * attended.astype(jnp.float32), -1)
    query_gradient = jnp.zeros((TOKEN_COUNT, HEAD_WIDTH), jnp.float32)
    key_gradient = jnp.zeros((TOKEN_COUNT, HEAD_WIDTH), jnp.float32)
    value_gradient = jnp.zeros((TOKEN_COUNT, HEAD_WIDTH), jnp.float32)
    for dilation_rate, start_offset, segs, query_rows_local, key_rows_local, value_rows_local, gradient_rows, logit_score in levels:
        lse_rows = pick_rows(lse, dilation_rate, start_offset).reshape(segs, -1)
        delta_rows = pick_rows(delta, dilation_rate, start_offset).reshape(segs, -1)
        probability = jnp.exp(logit_score - lse_rows[..., None])
        probability_gradient = jnp.einsum('lrz,laz->lra', gradient_rows, value_rows_local)
        score_gradient = rounded_length(probability * (probability_gradient - delta_rows[..., None]))
        query_gradient = scatter_rows(query_gradient, (softmax_scale * jnp.einsum('rtg,rgi->rti', score_gradient, key_rows_local)).reshape(-1, HEAD_WIDTH), dilation_rate, start_offset, jnp.add)
        key_gradient = scatter_rows(key_gradient, (softmax_scale * jnp.einsum('nry,nrz->nyz', score_gradient, query_rows_local)).reshape(-1, HEAD_WIDTH), dilation_rate, start_offset, jnp.add)
        value_gradient = scatter_rows(value_gradient, jnp.einsum('nry,nrz->nyz', rounded_length(probability), gradient_rows).reshape(-1, HEAD_WIDTH), dilation_rate, start_offset, jnp.add)
    return attended, query_gradient.astype(jnp.bfloat16), key_gradient.astype(jnp.bfloat16), value_gradient.astype(jnp.bfloat16)


def reference(query, key, value, out_grad, offsets):
    def heads_first(values):
        return values.reshape(TOKEN_COUNT, HEADS, HEAD_WIDTH).transpose(1, 0, 2)

    def tokens_first(values):
        return values.transpose(1, 0, 2).reshape(TOKEN_COUNT, HEADS * HEAD_WIDTH)

    results = lax.map(one_head, (heads_first(query), heads_first(key), heads_first(value), heads_first(out_grad), offsets[0], offsets[1]))
    return (tokens_first(results[0]), tokens_first(results[1]), tokens_first(results[2]), tokens_first(results[3]))
```

```python
import functools
import math

import jax
import jax.numpy as jnp
from jax import lax
from jax.experimental import pallas as pl
from jax.experimental.pallas import tpu as pltpu
from jax.sharding import PartitionSpec as P

MIDDLE_DILATION = 16
UPPER_DILATION = 64
MIDDLE_SEGMENTS = 4
LOWEST = -1e30
MESH = pl.DeviceIdType.MESH
F32 = jnp.float32
BF16 = jnp.bfloat16


def contract(a, b, dim_a, dim_b):
    return lax.dot_general(a, b, (((dim_a,), (dim_b,)), ((), ())), preferred_element_type=F32)


def one_hot(shape, row_dim, tok, middle_offset, upper_offset, copies):
    mid_rows, top_rows = tok // MIDDLE_DILATION, tok // UPPER_DILATION
    rows = lax.broadcasted_iota(jnp.int32, shape, row_dim)
    token = lax.broadcasted_iota(jnp.int32, shape, 1 - row_dim)
    if copies > 1:
        rows = jnp.where(rows >= mid_rows + top_rows, rows - (mid_rows + top_rows), rows)
    owner = jnp.where(
        rows < mid_rows,
        rows * MIDDLE_DILATION + middle_offset,
        (rows - mid_rows) * UPPER_DILATION + upper_offset,
    )
    return jnp.where(token == owner, 1.0, 0.0).astype(BF16)


def kernel(
    dims,
    offsets, query, key, value, out_grad,
    attended_out, query_out, key_out, value_out,
    arrived, staged, partial,
    mid_own, mid_rows_in, top_own, top_rows_in,
    mid_back, mid_back_in, top_back, top_back_in,
    in_recv, mid_recv, top_recv, mid_back_recv, top_back_recv, out_recv,
    in_send, mid_send, top_send, mid_back_send, top_back_send, out_send,
):
    ctx_count, mid_count, group, heads, own_rows, width = dims
    tok = own_rows * group
    mid_n, top_n = tok // MIDDLE_DILATION, tok // UPPER_DILATION
    ctx, me = lax.axis_index("ctx"), lax.axis_index("head")
    mid_base = ctx // mid_count * mid_count
    mid_me = ctx % mid_count
    sources = (query, key, value, out_grad)
    results = (attended_out, query_out, key_out, value_out)
    scale = width ** -0.5

    barrier = pltpu.get_barrier_semaphore()
    for step in range(1, group):
        pl.semaphore_signal(barrier, inc=1, device_id={"head": (me + step) % group}, device_id_type=MESH)

    def greet(step, carry):
        pl.semaphore_signal(barrier, inc=1, device_id={"ctx": (ctx + step) % ctx_count}, device_id_type=MESH)
        return carry

    lax.fori_loop(1, ctx_count, greet, 0)
    pl.semaphore_wait(barrier, group - 1 + ctx_count - 1)

    def columns(device, head):
        return pl.ds(pl.multiple_of((device * heads + head) * width, width), width)

    def rows_of(device):
        return pl.ds(pl.multiple_of(device * own_rows, own_rows), own_rows)

    def send_in(head, carry):
        for step in range(group):
            device = (me + step) % group
            for a in (1, 2, 0, 3):
                src = sources[a].at[:, columns(device, head)]
                dst = arrived.at[head, a, rows_of(me)]
                if step == 0:
                    pltpu.make_async_copy(src, dst, in_recv.at[head]).start()
                else:
                    pltpu.make_async_remote_copy(
                        src, dst, in_send.at[a], in_recv.at[head],
                        device_id={"head": device}, device_id_type=MESH,
                    ).start()
        return carry

    lax.fori_loop(0, heads, send_in, 0)

    def ring(count, place, base, src_of, dst, send_sem, recv_sem):
        def body(step, carry):
            other = (place + step) % count
            pltpu.make_async_remote_copy(
                src_of(other), dst, send_sem, recv_sem,
                device_id={"ctx": base + other}, device_id_type=MESH,
            ).start()
            return carry

        lax.fori_loop(1, count, body, 0)

    def wait_for(ref, sem):
        pltpu.make_async_copy(ref, ref, sem).wait()

    def gather_rows(head):
        wait_for(arrived.at[head], in_recv.at[head])
        pick = one_hot((mid_n + top_n, tok), 0, tok, offsets[0, head], offsets[1, head], 1)
        key_rows = contract(pick, arrived[head, 1], 1, 0)
        value_rows = contract(pick, arrived[head, 2], 1, 0)
        mid = jnp.concatenate([key_rows[:mid_n], value_rows[:mid_n]], 0).astype(BF16)
        top = jnp.concatenate([key_rows[mid_n:], value_rows[mid_n:]], 0).astype(BF16)
        mid_own[head] = mid
        top_own[head] = top
        mid_rows_in[head, mid_me] = mid
        top_rows_in[head, ctx] = top
        ring(ctx_count, ctx, 0, lambda other: top_own.at[head], top_rows_in.at[head, ctx],
             top_send, top_recv.at[head])
        ring(mid_count, mid_me, mid_base, lambda other: mid_own.at[head], mid_rows_in.at[head, mid_me],
             mid_send, mid_recv.at[head])

    def send_out(head, a):
        for step in range(group):
            device = (me + step) % group
            src = staged.at[head, a, rows_of(device)]
            dst = results[a].at[:, columns(me, head)]
            if step == 0:
                pltpu.make_async_copy(src, dst, out_recv.at[a]).start()
            else:
                pltpu.make_async_remote_copy(
                    src, dst, out_send.at[a], out_recv.at[a],
                    device_id={"head": device}, device_id_type=MESH,
                ).start()

    def attend(head):
        wait_for(mid_rows_in.at[head, pl.ds(0, mid_count - 1)], mid_recv.at[head])
        wait_for(top_rows_in.at[head, pl.ds(0, ctx_count - 1)], top_recv.at[head])
        mid_in = mid_rows_in[head].astype(F32)
        top_in = top_rows_in[head].astype(F32)
        mid_all, top_all = mid_count * mid_n, ctx_count * top_n
        q, do = arrived[head, 0], arrived[head, 3]
        k = jnp.concatenate([
            arrived[head, 1],
            mid_in[:, :mid_n].reshape(mid_all, width).astype(BF16),
            top_in[:, :top_n].reshape(top_all, width).astype(BF16),
        ], 0)
        v = jnp.concatenate([
            arrived[head, 2],
            mid_in[:, mid_n:].reshape(mid_all, width).astype(BF16),
            top_in[:, top_n:].reshape(top_all, width).astype(BF16),
        ], 0)
        position = lax.broadcasted_iota(jnp.int32, (1, tok), 1)
        in_mid = position % MIDDLE_DILATION == offsets[0, head]
        in_top = position % UPPER_DILATION == offsets[1, head]
        score = contract(k, q, 1, 1) * (scale * math.log2(math.e))
        score = jnp.concatenate([
            score[:tok],
            jnp.where(in_mid, score[tok:tok + mid_all], LOWEST),
            jnp.where(in_top, score[tok + mid_all:], LOWEST),
        ], 0)
        top = jnp.max(score, 0, keepdims=True)
        weight = jnp.exp2(score - top)
        inverse = 1.0 / jnp.sum(weight, 0, keepdims=True)
        attended = (contract(v, weight.astype(BF16), 0, 0) * inverse).astype(BF16).astype(F32)
        delta = jnp.sum(do.astype(F32).T * attended, 0, keepdims=True)
        prob = weight * inverse
        dscore = (prob * (contract(v, do, 1, 1) - delta)).astype(BF16)
        staged[head, 0] = attended.T.astype(BF16)
        send_out(head, 0)
        staged[head, 1] = (contract(k, dscore, 0, 0) * scale).T.astype(BF16)
        send_out(head, 1)
        dk = contract(dscore, q, 1, 0) * scale
        dv = contract(prob.astype(BF16), do, 1, 0)
        partial[head % 2, 0] = dk[:tok]
        partial[head % 2, 1] = dv[:tok]

        def both(low, count, n):
            return jnp.concatenate([
                dk[low:low + count * n].reshape(count, n, width),
                dv[low:low + count * n].reshape(count, n, width),
            ], 1).astype(BF16)

        mid_back[head] = both(tok, mid_count, mid_n)
        top_back[head] = both(tok + mid_all, ctx_count, top_n)
        ring(ctx_count, ctx, 0, lambda other: top_back.at[head, other], top_back_in.at[head, ctx],
             top_back_send, top_back_recv.at[head])
        ring(mid_count, mid_me, mid_base, lambda other: mid_back.at[head, other], mid_back_in.at[head, mid_me],
             mid_back_send, mid_back_recv.at[head])
        top_back_in[head, ctx] = top_back[head, ctx]
        mid_back_in[head, mid_me] = mid_back[head, mid_me]

    def finish(head):
        wait_for(mid_back_in.at[head, pl.ds(0, mid_count - 1)], mid_back_recv.at[head])
        wait_for(top_back_in.at[head, pl.ds(0, ctx_count - 1)], top_back_recv.at[head])
        mid = jnp.sum(mid_back_in[head].astype(F32), 0)
        top = jnp.sum(top_back_in[head].astype(F32), 0)
        rows = jnp.concatenate([
            jnp.concatenate([mid[:mid_n], top[:top_n]], 0),
            jnp.concatenate([mid[mid_n:], top[top_n:]], 0),
        ], 1)
        high = rows.astype(BF16).astype(F32)
        both = jnp.concatenate([high, rows - high], 0).astype(BF16)
        place = one_hot((tok, 2 * (mid_n + top_n)), 1, tok, offsets[0, head], offsets[1, head], 2)
        added = contract(place, both, 1, 0)
        staged[head, 2] = (partial[head % 2, 0] + added[:, :width]).astype(BF16)
        send_out(head, 2)
        staged[head, 3] = (partial[head % 2, 1] + added[:, width:]).astype(BF16)
        send_out(head, 3)

    gather_rows(0)

    def turn(head, carry):
        @pl.when(head < heads - 1)
        def _():
            gather_rows(head + 1)

        attend(head)

        @pl.when(head > 0)
        def _():
            finish(head - 1)

        return carry

    lax.fori_loop(0, heads, turn, 0)
    finish(heads - 1)

    others = pl.ds(0, own_rows * (group - 1))
    for a in range(4):
        wait_for(results[a], out_recv.at[a])
        wait_for(staged.at[:, a, others], out_send.at[a])
        wait_for(arrived.at[:, a, others], in_send.at[a])
    wait_for(mid_rows_in.at[:, pl.ds(0, mid_count - 1)], mid_send)
    wait_for(top_rows_in.at[:, pl.ds(0, ctx_count - 1)], top_send)
    wait_for(mid_back_in.at[:, pl.ds(0, mid_count - 1)], mid_back_send)
    wait_for(top_back_in.at[:, pl.ds(0, ctx_count - 1)], top_back_send)


def local(query, key, value, out_grad, offsets):
    ctx_count, group = lax.axis_size("ctx"), lax.axis_size("head")
    heads = offsets.shape[1]
    own_rows = query.shape[0]
    width = query.shape[1] // (group * heads)
    tok = own_rows * group
    mid_count = ctx_count // MIDDLE_SEGMENTS
    mid_n, top_n = tok // MIDDLE_DILATION, tok // UPPER_DILATION
    dims = (ctx_count, mid_count, group, heads, own_rows, width)
    anywhere = pl.BlockSpec(memory_space=pl.ANY)
    dma = pltpu.SemaphoreType.DMA
    return pl.pallas_call(
        functools.partial(kernel, dims),
        out_shape=tuple(jax.ShapeDtypeStruct(query.shape, BF16) for _ in range(4)),
        in_specs=[pl.BlockSpec(memory_space=pltpu.SMEM)] + [anywhere] * 4,
        out_specs=(anywhere,) * 4,
        scratch_shapes=[
            pltpu.VMEM((heads, 4, tok, width), BF16),
            pltpu.VMEM((heads, 4, tok, width), BF16),
            pltpu.VMEM((2, 2, tok, width), F32),
            pltpu.VMEM((heads, 2 * mid_n, width), BF16),
            pltpu.VMEM((heads, mid_count, 2 * mid_n, width), BF16),
            pltpu.VMEM((heads, 2 * top_n, width), BF16),
            pltpu.VMEM((heads, ctx_count, 2 * top_n, width), BF16),
            pltpu.VMEM((heads, mid_count, 2 * mid_n, width), BF16),
            pltpu.VMEM((heads, mid_count, 2 * mid_n, width), BF16),
            pltpu.VMEM((heads, ctx_count, 2 * top_n, width), BF16),
            pltpu.VMEM((heads, ctx_count, 2 * top_n, width), BF16),
            dma((heads,)), dma((heads,)), dma((heads,)), dma((heads,)), dma((heads,)), dma((4,)),
            dma((4,)), dma, dma, dma, dma, dma((4,)),
        ],
        compiler_params=pltpu.CompilerParams(
            collective_id=0, has_side_effects=True, vmem_limit_bytes=56 * 1024 * 1024
        ),
        cost_estimate=pl.CostEstimate(
            flops=12 * heads * tok * (tok + 128) * width,
            bytes_accessed=16 * query.size,
            transcendentals=heads * tok * (tok + 128),
        ),
        name="dilated_attention",
    )(offsets, query, key, value, out_grad)


def solution(mesh):
    rows = P(("ctx", "head"), None)
    return jax.shard_map(
        local, mesh=mesh, in_specs=(rows,) * 4 + (P(None, "head"),), out_specs=(rows,) * 4, check_vma=False
    )
```

```python
import functools
import math

import jax
import jax.numpy as jnp
from jax import lax
from jax.experimental import pallas as pl
from jax.experimental.pallas import tpu as pltpu
from jax.sharding import PartitionSpec as P

MIDDLE_DILATION = 16
UPPER_DILATION = 64
MIDDLE_SEGMENTS = 4
LOWEST = -1e30
HELD_BACK = 3
MESH = pl.DeviceIdType.MESH
F32 = jnp.float32
BF16 = jnp.bfloat16


def contract(a, b, dim_a, dim_b):
    return lax.dot_general(a, b, (((dim_a,), (dim_b,)), ((), ())), preferred_element_type=F32)


def one_hot(shape, row_dim, tok, middle_offset, upper_offset, copies):
    mid_rows, top_rows = tok // MIDDLE_DILATION, tok // UPPER_DILATION
    rows = lax.broadcasted_iota(jnp.int32, shape, row_dim)
    token = lax.broadcasted_iota(jnp.int32, shape, 1 - row_dim)
    if copies > 1:
        rows = jnp.where(rows >= mid_rows + top_rows, rows - (mid_rows + top_rows), rows)
    owner = jnp.where(
        rows < mid_rows,
        rows * MIDDLE_DILATION + middle_offset,
        (rows - mid_rows) * UPPER_DILATION + upper_offset,
    )
    return jnp.where(token == owner, 1.0, 0.0).astype(BF16)


def kernel(
    dims,
    offsets, query, key, value, out_grad,
    attended_out, query_out, key_out, value_out,
    arrived, staged, partial,
    mid_own, mid_rows_in, top_own, top_rows_in,
    mid_back, mid_back_in, top_back, top_back_in,
    in_recv, mid_recv, top_recv, mid_back_recv, top_back_recv, out_recv,
    in_send, mid_send, top_send, mid_back_send, top_back_send, out_send,
):
    ctx_count, mid_count, group, heads, own_rows, width = dims
    tok = own_rows * group
    mid_n, top_n = tok // MIDDLE_DILATION, tok // UPPER_DILATION
    ctx, me = lax.axis_index("ctx"), lax.axis_index("head")
    mid_base = ctx // mid_count * mid_count
    mid_me = ctx % mid_count
    sources = (query, key, value, out_grad)
    results = (attended_out, query_out, key_out, value_out)
    scale = width ** -0.5
    held = max(heads - HELD_BACK, 1)

    barrier = pltpu.get_barrier_semaphore()
    for step in range(1, group):
        pl.semaphore_signal(barrier, inc=1, device_id={"head": (me + step) % group}, device_id_type=MESH)

    def greet(step, carry):
        pl.semaphore_signal(barrier, inc=1, device_id={"ctx": (ctx + step) % ctx_count}, device_id_type=MESH)
        return carry

    lax.fori_loop(1, ctx_count, greet, 0)
    pl.semaphore_wait(barrier, group - 1 + ctx_count - 1)

    def columns(device, head):
        return pl.ds(pl.multiple_of((device * heads + head) * width, width), width)

    def rows_of(device):
        return pl.ds(pl.multiple_of(device * own_rows, own_rows), own_rows)

    def send_in(head, carry):
        for step in range(group):
            device = (me + step) % group
            for a in (1, 2, 0, 3):
                src = sources[a].at[:, columns(device, head)]
                dst = arrived.at[head, a, rows_of(me)]
                if step == 0:
                    pltpu.make_async_copy(src, dst, in_recv.at[head]).start()
                else:
                    pltpu.make_async_remote_copy(
                        src, dst, in_send.at[a], in_recv.at[head],
                        device_id={"head": device}, device_id_type=MESH,
                    ).start()
        return carry

    lax.fori_loop(0, heads, send_in, 0)

    def ring(count, place, base, src_of, dst, send_sem, recv_sem):
        def body(step, carry):
            other = (place + step) % count
            pltpu.make_async_remote_copy(
                src_of(other), dst, send_sem, recv_sem,
                device_id={"ctx": base + other}, device_id_type=MESH,
            ).start()
            return carry

        lax.fori_loop(1, count, body, 0)

    def wait_for(ref, sem):
        pltpu.make_async_copy(ref, ref, sem).wait()

    def gather_rows(head):
        wait_for(arrived.at[head], in_recv.at[head])
        pick = one_hot((mid_n + top_n, tok), 0, tok, offsets[0, head], offsets[1, head], 1)
        key_rows = contract(pick, arrived[head, 1], 1, 0)
        value_rows = contract(pick, arrived[head, 2], 1, 0)
        mid = jnp.concatenate([key_rows[:mid_n], value_rows[:mid_n]], 0).astype(BF16)
        top = jnp.concatenate([key_rows[mid_n:], value_rows[mid_n:]], 0).astype(BF16)
        mid_own[head] = mid
        top_own[head] = top
        mid_rows_in[head, mid_me] = mid
        top_rows_in[head, ctx] = top
        ring(ctx_count, ctx, 0, lambda other: top_own.at[head], top_rows_in.at[head, ctx],
             top_send, top_recv.at[head])
        ring(mid_count, mid_me, mid_base, lambda other: mid_own.at[head], mid_rows_in.at[head, mid_me],
             mid_send, mid_recv.at[head])

    def send_out(head, a):
        for step in range(group):
            device = (me + step) % group
            src = staged.at[head, a, rows_of(device)]
            dst = results[a].at[:, columns(me, head)]
            if step == 0:
                pltpu.make_async_copy(src, dst, out_recv.at[a]).start()
            else:
                pltpu.make_async_remote_copy(
                    src, dst, out_send.at[a], out_recv.at[a],
                    device_id={"head": device}, device_id_type=MESH,
                ).start()

    def send_unless_held(head, a):
        @pl.when(head >= held)
        def _():
            send_out(head, a)

    def attend(head):
        wait_for(mid_rows_in.at[head, pl.ds(0, mid_count - 1)], mid_recv.at[head])
        wait_for(top_rows_in.at[head, pl.ds(0, ctx_count - 1)], top_recv.at[head])
        mid_in = mid_rows_in[head].astype(F32)
        top_in = top_rows_in[head].astype(F32)
        mid_all, top_all = mid_count * mid_n, ctx_count * top_n
        q, do = arrived[head, 0], arrived[head, 3]
        k = jnp.concatenate([
            arrived[head, 1],
            mid_in[:, :mid_n].reshape(mid_all, width).astype(BF16),
            top_in[:, :top_n].reshape(top_all, width).astype(BF16),
        ], 0)
        v = jnp.concatenate([
            arrived[head, 2],
            mid_in[:, mid_n:].reshape(mid_all, width).astype(BF16),
            top_in[:, top_n:].reshape(top_all, width).astype(BF16),
        ], 0)
        position = lax.broadcasted_iota(jnp.int32, (1, tok), 1)
        in_mid = position % MIDDLE_DILATION == offsets[0, head]
        in_top = position % UPPER_DILATION == offsets[1, head]
        score = contract(k, q, 1, 1) * (scale * math.log2(math.e))
        score = jnp.concatenate([
            score[:tok],
            jnp.where(in_mid, score[tok:tok + mid_all], LOWEST),
            jnp.where(in_top, score[tok + mid_all:], LOWEST),
        ], 0)
        top = jnp.max(score, 0, keepdims=True)
        weight = jnp.exp2(score - top)
        inverse = 1.0 / jnp.sum(weight, 0, keepdims=True)
        attended = (contract(v, weight.astype(BF16), 0, 0) * inverse).astype(BF16).astype(F32)
        delta = jnp.sum(do.astype(F32).T * attended, 0, keepdims=True)
        prob = weight * inverse
        dscore = (prob * (contract(v, do, 1, 1) - delta)).astype(BF16)
        staged[head, 0] = attended.T.astype(BF16)
        send_unless_held(head, 0)
        staged[head, 1] = (contract(k, dscore, 0, 0) * scale).T.astype(BF16)
        send_unless_held(head, 1)
        dk = contract(dscore, q, 1, 0) * scale
        dv = contract(prob.astype(BF16), do, 1, 0)
        partial[head % 2, 0] = dk[:tok]
        partial[head % 2, 1] = dv[:tok]

        def both(low, count, n):
            return jnp.concatenate([
                dk[low:low + count * n].reshape(count, n, width),
                dv[low:low + count * n].reshape(count, n, width),
            ], 1).astype(BF16)

        mid_back[head] = both(tok, mid_count, mid_n)
        top_back[head] = both(tok + mid_all, ctx_count, top_n)
        ring(ctx_count, ctx, 0, lambda other: top_back.at[head, other], top_back_in.at[head, ctx],
             top_back_send, top_back_recv.at[head])
        ring(mid_count, mid_me, mid_base, lambda other: mid_back.at[head, other], mid_back_in.at[head, mid_me],
             mid_back_send, mid_back_recv.at[head])
        top_back_in[head, ctx] = top_back[head, ctx]
        mid_back_in[head, mid_me] = mid_back[head, mid_me]

    def finish(head):
        wait_for(mid_back_in.at[head, pl.ds(0, mid_count - 1)], mid_back_recv.at[head])
        wait_for(top_back_in.at[head, pl.ds(0, ctx_count - 1)], top_back_recv.at[head])
        mid = jnp.sum(mid_back_in[head].astype(F32), 0)
        top = jnp.sum(top_back_in[head].astype(F32), 0)
        rows = jnp.concatenate([
            jnp.concatenate([mid[:mid_n], top[:top_n]], 0),
            jnp.concatenate([mid[mid_n:], top[top_n:]], 0),
        ], 1)
        high = rows.astype(BF16).astype(F32)
        both = jnp.concatenate([high, rows - high], 0).astype(BF16)
        place = one_hot((tok, 2 * (mid_n + top_n)), 1, tok, offsets[0, head], offsets[1, head], 2)
        added = contract(place, both, 1, 0)
        staged[head, 2] = (partial[head % 2, 0] + added[:, :width]).astype(BF16)
        send_unless_held(head, 2)
        staged[head, 3] = (partial[head % 2, 1] + added[:, width:]).astype(BF16)
        send_unless_held(head, 3)

    def release(head, carry):
        for a in range(4):
            send_out(head, a)
        return carry

    gather_rows(0)

    def turn(head, carry):
        @pl.when(head < heads - 1)
        def _():
            gather_rows(head + 1)

        attend(head)

        @pl.when(head > 0)
        def _():
            finish(head - 1)

        @pl.when(head == held)
        def _():
            lax.fori_loop(0, held, release, 0)

        return carry

    lax.fori_loop(0, heads, turn, 0)
    finish(heads - 1)

    others = pl.ds(0, own_rows * (group - 1))
    for a in range(4):
        wait_for(results[a], out_recv.at[a])
        wait_for(staged.at[:, a, others], out_send.at[a])
        wait_for(arrived.at[:, a, others], in_send.at[a])
    wait_for(mid_rows_in.at[:, pl.ds(0, mid_count - 1)], mid_send)
    wait_for(top_rows_in.at[:, pl.ds(0, ctx_count - 1)], top_send)
    wait_for(mid_back_in.at[:, pl.ds(0, mid_count - 1)], mid_back_send)
    wait_for(top_back_in.at[:, pl.ds(0, ctx_count - 1)], top_back_send)


def hand_over(*refs):
    sources, results, sem = refs[:4], refs[4:8], refs[8]
    copies = [pltpu.make_async_copy(src, dst, sem.at[i]) for i, (src, dst) in enumerate(zip(sources, results))]
    for copy in copies:
        copy.start()
    for copy in copies:
        copy.wait()


def local(query, key, value, out_grad, offsets):
    ctx_count, group = lax.axis_size("ctx"), lax.axis_size("head")
    heads = offsets.shape[1]
    own_rows = query.shape[0]
    width = query.shape[1] // (group * heads)
    tok = own_rows * group
    mid_count = ctx_count // MIDDLE_SEGMENTS
    mid_n, top_n = tok // MIDDLE_DILATION, tok // UPPER_DILATION
    dims = (ctx_count, mid_count, group, heads, own_rows, width)
    anywhere = pl.BlockSpec(memory_space=pl.ANY)
    dma = pltpu.SemaphoreType.DMA
    landed = pl.pallas_call(
        functools.partial(kernel, dims),
        out_shape=tuple(pltpu.VMEM(query.shape, BF16) for _ in range(4)),
        in_specs=[pl.BlockSpec(memory_space=pltpu.SMEM)] + [anywhere] * 4,
        out_specs=(anywhere,) * 4,
        scratch_shapes=[
            pltpu.VMEM((heads, 4, tok, width), BF16),
            pltpu.VMEM((heads, 4, tok, width), BF16),
            pltpu.VMEM((2, 2, tok, width), F32),
            pltpu.VMEM((heads, 2 * mid_n, width), BF16),
            pltpu.VMEM((heads, mid_count, 2 * mid_n, width), BF16),
            pltpu.VMEM((heads, 2 * top_n, width), BF16),
            pltpu.VMEM((heads, ctx_count, 2 * top_n, width), BF16),
            pltpu.VMEM((heads, mid_count, 2 * mid_n, width), BF16),
            pltpu.VMEM((heads, mid_count, 2 * mid_n, width), BF16),
            pltpu.VMEM((heads, ctx_count, 2 * top_n, width), BF16),
            pltpu.VMEM((heads, ctx_count, 2 * top_n, width), BF16),
            dma((heads,)), dma((heads,)), dma((heads,)), dma((heads,)), dma((heads,)), dma((4,)),
            dma((4,)), dma, dma, dma, dma, dma((4,)),
        ],
        compiler_params=pltpu.CompilerParams(
            collective_id=0, has_side_effects=True, vmem_limit_bytes=56 * 1024 * 1024
        ),
        cost_estimate=pl.CostEstimate(
            flops=12 * heads * tok * (tok + 128) * width,
            bytes_accessed=16 * query.size,
            transcendentals=heads * tok * (tok + 128),
        ),
        name="dilated_attention",
    )(offsets, query, key, value, out_grad)
    return pl.pallas_call(
        hand_over,
        out_shape=tuple(jax.ShapeDtypeStruct(query.shape, BF16) for _ in range(4)),
        in_specs=[anywhere] * 4,
        out_specs=(anywhere,) * 4,
        scratch_shapes=[dma((4,))],
        name="hand_over",
    )(*landed)


def solution(mesh):
    rows = P(("ctx", "head"), None)
    return jax.shard_map(
        local, mesh=mesh, in_specs=(rows,) * 4 + (P(None, "head"),), out_specs=(rows,) * 4, check_vma=False
    )
```

```python
import functools
import math

import jax
import jax.numpy as jnp
from jax import lax
from jax.experimental import pallas as pl
from jax.experimental.pallas import tpu as pltpu
from jax.sharding import PartitionSpec as P

MIDDLE_DILATION = 16
UPPER_DILATION = 64
MIDDLE_SEGMENTS = 4
LOWEST = -1e30
MESH = pl.DeviceIdType.MESH
F32 = jnp.float32
BF16 = jnp.bfloat16


def contract(a, b, dim_a, dim_b):
    return lax.dot_general(a, b, (((dim_a,), (dim_b,)), ((), ())), preferred_element_type=F32)


def one_hot(shape, row_dim, tok, middle_offset, upper_offset, copies):
    mid_rows, top_rows = tok // MIDDLE_DILATION, tok // UPPER_DILATION
    rows = lax.broadcasted_iota(jnp.int32, shape, row_dim)
    token = lax.broadcasted_iota(jnp.int32, shape, 1 - row_dim)
    if copies > 1:
        rows = jnp.where(rows >= mid_rows + top_rows, rows - (mid_rows + top_rows), rows)
    owner = jnp.where(
        rows < mid_rows,
        rows * MIDDLE_DILATION + middle_offset,
        (rows - mid_rows) * UPPER_DILATION + upper_offset,
    )
    return jnp.where(token == owner, 1.0, 0.0).astype(BF16)


def kernel(
    dims,
    offsets, query, key, value, out_grad,
    attended_out, query_out, key_out, value_out,
    arrived, staged, partial,
    mid_own, mid_rows_in, top_own, top_rows_in,
    mid_back, mid_back_in, top_back, top_back_in,
    in_recv, mid_recv, top_recv, mid_back_recv, top_back_recv, out_recv,
    in_send, mid_send, top_send, mid_back_send, top_back_send, out_send, entered,
):
    ctx_count, mid_count, group, heads, own_rows, width = dims
    tok = own_rows * group
    mid_n, top_n = tok // MIDDLE_DILATION, tok // UPPER_DILATION
    ctx, me = lax.axis_index("ctx"), lax.axis_index("head")
    mid_base = ctx // mid_count * mid_count
    mid_me = ctx % mid_count
    sources = (query, key, value, out_grad)
    results = (attended_out, query_out, key_out, value_out)
    scale = width ** -0.5

    def signal_ctx(sem, low, high):
        def body(other, carry):
            pl.semaphore_signal(sem, inc=1, device_id={"ctx": other}, device_id_type=MESH)
            return carry

        lax.fori_loop(low, high, body, 0)

    barrier = pltpu.get_barrier_semaphore()
    for step in range(1, group):
        pl.semaphore_signal(barrier, inc=1, device_id={"head": (me + step) % group}, device_id_type=MESH)
    signal_ctx(barrier, ctx + 1, ctx_count)
    pl.semaphore_wait(barrier, group - 1 + ctx)

    def columns(device, head):
        return pl.ds(pl.multiple_of((device * heads + head) * width, width), width)

    def rows_of(device):
        return pl.ds(pl.multiple_of(device * own_rows, own_rows), own_rows)

    def send_in(head, carry):
        for step in range(group):
            device = (me + step) % group
            for a in (1, 2, 0, 3):
                src = sources[a].at[:, columns(device, head)]
                dst = arrived.at[head, a, rows_of(me)]
                if step == 0:
                    pltpu.make_async_copy(src, dst, in_recv.at[head]).start()
                else:
                    pltpu.make_async_remote_copy(
                        src, dst, in_send.at[a], in_recv.at[head],
                        device_id={"head": device}, device_id_type=MESH,
                    ).start()
        return carry

    lax.fori_loop(0, heads, send_in, 0)
    signal_ctx(entered, 0, ctx)

    @pl.when(ctx < ctx_count - 1)
    def _():
        pl.semaphore_wait(entered, ctx_count - 1 - ctx)

    def ring(count, place, base, src_of, dst, send_sem, recv_sem):
        def body(step, carry):
            other = (place + step) % count
            pltpu.make_async_remote_copy(
                src_of(other), dst, send_sem, recv_sem,
                device_id={"ctx": base + other}, device_id_type=MESH,
            ).start()
            return carry

        lax.fori_loop(1, count, body, 0)

    def wait_for(ref, sem):
        pltpu.make_async_copy(ref, ref, sem).wait()

    def gather_rows(head):
        wait_for(arrived.at[head], in_recv.at[head])
        pick = one_hot((mid_n + top_n, tok), 0, tok, offsets[0, head], offsets[1, head], 1)
        key_rows = contract(pick, arrived[head, 1], 1, 0)
        value_rows = contract(pick, arrived[head, 2], 1, 0)
        mid = jnp.concatenate([key_rows[:mid_n], value_rows[:mid_n]], 0).astype(BF16)
        top = jnp.concatenate([key_rows[mid_n:], value_rows[mid_n:]], 0).astype(BF16)
        mid_own[head] = mid
        top_own[head] = top
        mid_rows_in[head, mid_me] = mid
        top_rows_in[head, ctx] = top
        ring(ctx_count, ctx, 0, lambda other: top_own.at[head], top_rows_in.at[head, ctx],
             top_send, top_recv.at[head])
        ring(mid_count, mid_me, mid_base, lambda other: mid_own.at[head], mid_rows_in.at[head, mid_me],
             mid_send, mid_recv.at[head])

    def send_out(head, a):
        for step in range(group):
            device = (me + step) % group
            src = staged.at[head, a, rows_of(device)]
            dst = results[a].at[:, columns(me, head)]
            if step == 0:
                pltpu.make_async_copy(src, dst, out_recv.at[a]).start()
            else:
                pltpu.make_async_remote_copy(
                    src, dst, out_send.at[a], out_recv.at[a],
                    device_id={"head": device}, device_id_type=MESH,
                ).start()

    def attend(head):
        wait_for(mid_rows_in.at[head, pl.ds(0, mid_count - 1)], mid_recv.at[head])
        wait_for(top_rows_in.at[head, pl.ds(0, ctx_count - 1)], top_recv.at[head])
        mid_in = mid_rows_in[head].astype(F32)
        top_in = top_rows_in[head].astype(F32)
        mid_all, top_all = mid_count * mid_n, ctx_count * top_n
        q, do = arrived[head, 0], arrived[head, 3]
        k = jnp.concatenate([
            arrived[head, 1],
            mid_in[:, :mid_n].reshape(mid_all, width).astype(BF16),
            top_in[:, :top_n].reshape(top_all, width).astype(BF16),
        ], 0)
        v = jnp.concatenate([
            arrived[head, 2],
            mid_in[:, mid_n:].reshape(mid_all, width).astype(BF16),
            top_in[:, top_n:].reshape(top_all, width).astype(BF16),
        ], 0)
        position = lax.broadcasted_iota(jnp.int32, (1, tok), 1)
        in_mid = position % MIDDLE_DILATION == offsets[0, head]
        in_top = position % UPPER_DILATION == offsets[1, head]
        score = contract(k, q, 1, 1) * (scale * math.log2(math.e))
        score = jnp.concatenate([
            score[:tok],
            jnp.where(in_mid, score[tok:tok + mid_all], LOWEST),
            jnp.where(in_top, score[tok + mid_all:], LOWEST),
        ], 0)
        top = jnp.max(score, 0, keepdims=True)
        weight = jnp.exp2(score - top)
        inverse = 1.0 / jnp.sum(weight, 0, keepdims=True)
        attended = (contract(v, weight.astype(BF16), 0, 0) * inverse).astype(BF16).astype(F32)
        delta = jnp.sum(do.astype(F32).T * attended, 0, keepdims=True)
        prob = weight * inverse
        dscore = (prob * (contract(v, do, 1, 1) - delta)).astype(BF16)
        staged[head, 0] = attended.T.astype(BF16)
        send_out(head, 0)
        staged[head, 1] = (contract(k, dscore, 0, 0) * scale).T.astype(BF16)
        send_out(head, 1)
        dk = contract(dscore, q, 1, 0) * scale
        dv = contract(prob.astype(BF16), do, 1, 0)
        partial[head % 2, 0] = dk[:tok]
        partial[head % 2, 1] = dv[:tok]

        def both(low, count, n):
            return jnp.concatenate([
                dk[low:low + count * n].reshape(count, n, width),
                dv[low:low + count * n].reshape(count, n, width),
            ], 1).astype(BF16)

        mid_back[head] = both(tok, mid_count, mid_n)
        top_back[head] = both(tok + mid_all, ctx_count, top_n)
        ring(ctx_count, ctx, 0, lambda other: top_back.at[head, other], top_back_in.at[head, ctx],
             top_back_send, top_back_recv.at[head])
        ring(mid_count, mid_me, mid_base, lambda other: mid_back.at[head, other], mid_back_in.at[head, mid_me],
             mid_back_send, mid_back_recv.at[head])
        top_back_in[head, ctx] = top_back[head, ctx]
        mid_back_in[head, mid_me] = mid_back[head, mid_me]

    def finish(head):
        wait_for(mid_back_in.at[head, pl.ds(0, mid_count - 1)], mid_back_recv.at[head])
        wait_for(top_back_in.at[head, pl.ds(0, ctx_count - 1)], top_back_recv.at[head])
        mid = jnp.sum(mid_back_in[head].astype(F32), 0)
        top = jnp.sum(top_back_in[head].astype(F32), 0)
        rows = jnp.concatenate([
            jnp.concatenate([mid[:mid_n], top[:top_n]], 0),
            jnp.concatenate([mid[mid_n:], top[top_n:]], 0),
        ], 1)
        high = rows.astype(BF16).astype(F32)
        both = jnp.concatenate([high, rows - high], 0).astype(BF16)
        place = one_hot((tok, 2 * (mid_n + top_n)), 1, tok, offsets[0, head], offsets[1, head], 2)
        added = contract(place, both, 1, 0)
        staged[head, 2] = (partial[head % 2, 0] + added[:, :width]).astype(BF16)
        send_out(head, 2)
        staged[head, 3] = (partial[head % 2, 1] + added[:, width:]).astype(BF16)
        send_out(head, 3)

    gather_rows(0)

    def turn(head, carry):
        @pl.when(head < heads - 1)
        def _():
            gather_rows(head + 1)

        attend(head)

        @pl.when(head > 0)
        def _():
            finish(head - 1)

        return carry

    lax.fori_loop(0, heads, turn, 0)
    finish(heads - 1)

    others = pl.ds(0, own_rows * (group - 1))
    for a in range(4):
        wait_for(results[a], out_recv.at[a])
        wait_for(staged.at[:, a, others], out_send.at[a])
        wait_for(arrived.at[:, a, others], in_send.at[a])
    wait_for(mid_rows_in.at[:, pl.ds(0, mid_count - 1)], mid_send)
    wait_for(top_rows_in.at[:, pl.ds(0, ctx_count - 1)], top_send)
    wait_for(mid_back_in.at[:, pl.ds(0, mid_count - 1)], mid_back_send)
    wait_for(top_back_in.at[:, pl.ds(0, ctx_count - 1)], top_back_send)


def hand_over(*refs):
    sources, results, sem = refs[:4], refs[4:8], refs[8]
    copies = [pltpu.make_async_copy(src, dst, sem.at[i]) for i, (src, dst) in enumerate(zip(sources, results))]
    for copy in copies:
        copy.start()
    for copy in copies:
        copy.wait()


def local(query, key, value, out_grad, offsets):
    ctx_count, group = lax.axis_size("ctx"), lax.axis_size("head")
    heads = offsets.shape[1]
    own_rows = query.shape[0]
    width = query.shape[1] // (group * heads)
    tok = own_rows * group
    mid_count = ctx_count // MIDDLE_SEGMENTS
    mid_n, top_n = tok // MIDDLE_DILATION, tok // UPPER_DILATION
    dims = (ctx_count, mid_count, group, heads, own_rows, width)
    anywhere = pl.BlockSpec(memory_space=pl.ANY)
    dma = pltpu.SemaphoreType.DMA
    landed = pl.pallas_call(
        functools.partial(kernel, dims),
        out_shape=tuple(pltpu.VMEM(query.shape, BF16) for _ in range(4)),
        in_specs=[pl.BlockSpec(memory_space=pltpu.SMEM)] + [anywhere] * 4,
        out_specs=(anywhere,) * 4,
        scratch_shapes=[
            pltpu.VMEM((heads, 4, tok, width), BF16),
            pltpu.VMEM((heads, 4, tok, width), BF16),
            pltpu.VMEM((2, 2, tok, width), F32),
            pltpu.VMEM((heads, 2 * mid_n, width), BF16),
            pltpu.VMEM((heads, mid_count, 2 * mid_n, width), BF16),
            pltpu.VMEM((heads, 2 * top_n, width), BF16),
            pltpu.VMEM((heads, ctx_count, 2 * top_n, width), BF16),
            pltpu.VMEM((heads, mid_count, 2 * mid_n, width), BF16),
            pltpu.VMEM((heads, mid_count, 2 * mid_n, width), BF16),
            pltpu.VMEM((heads, ctx_count, 2 * top_n, width), BF16),
            pltpu.VMEM((heads, ctx_count, 2 * top_n, width), BF16),
            dma((heads,)), dma((heads,)), dma((heads,)), dma((heads,)), dma((heads,)), dma((4,)),
            dma((4,)), dma, dma, dma, dma, dma((4,)), pltpu.SemaphoreType.REGULAR,
        ],
        compiler_params=pltpu.CompilerParams(
            collective_id=0, has_side_effects=True, vmem_limit_bytes=59 * 1024 * 1024
        ),
        cost_estimate=pl.CostEstimate(
            flops=12 * heads * tok * (tok + 128) * width,
            bytes_accessed=16 * query.size,
            transcendentals=heads * tok * (tok + 128),
        ),
        name="dilated_attention",
    )(offsets, query, key, value, out_grad)
    return pl.pallas_call(
        hand_over,
        out_shape=tuple(jax.ShapeDtypeStruct(query.shape, BF16) for _ in range(4)),
        in_specs=[anywhere] * 4,
        out_specs=(anywhere,) * 4,
        scratch_shapes=[dma((4,))],
        compiler_params=pltpu.CompilerParams(vmem_limit_bytes=16 * 1024 * 1024),
        name="hand_over",
    )(*(pltpu.with_memory_space_constraint(x, pltpu.VMEM) for x in landed))


def solution(mesh):
    rows = P(("ctx", "head"), None)
    return jax.shard_map(
        local, mesh=mesh, in_specs=(rows,) * 4 + (P(None, "head"),), out_specs=(rows,) * 4, check_vma=False
    )
```

```python
import functools
import math

import jax
import jax.numpy as jnp
from jax import lax
from jax.experimental import pallas as pl
from jax.experimental.pallas import tpu as pltpu
from jax.sharding import PartitionSpec as P

MIDDLE_DILATION = 16
UPPER_DILATION = 64
MIDDLE_SEGMENTS = 4
LOWEST = -1e30
BUNDLE = 2
MESH = pl.DeviceIdType.MESH
F32 = jnp.float32
BF16 = jnp.bfloat16


def contract(a, b, dim_a, dim_b):
    return lax.dot_general(a, b, (((dim_a,), (dim_b,)), ((), ())), preferred_element_type=F32)


def one_hot(shape, row_dim, tok, middle_offset, upper_offset, copies):
    mid_rows, top_rows = tok // MIDDLE_DILATION, tok // UPPER_DILATION
    rows = lax.broadcasted_iota(jnp.int32, shape, row_dim)
    token = lax.broadcasted_iota(jnp.int32, shape, 1 - row_dim)
    if copies > 1:
        rows = jnp.where(rows >= mid_rows + top_rows, rows - (mid_rows + top_rows), rows)
    owner = jnp.where(
        rows < mid_rows,
        rows * MIDDLE_DILATION + middle_offset,
        (rows - mid_rows) * UPPER_DILATION + upper_offset,
    )
    return jnp.where(token == owner, 1.0, 0.0).astype(BF16)


def kernel(
    dims,
    offsets, query, key, value, out_grad,
    attended_out, query_out, key_out, value_out,
    arrived, staged, partial,
    mid_own, mid_rows_in, top_own, top_rows_in,
    mid_back, mid_back_in, top_back, top_back_in,
    in_recv, mid_recv, top_recv, mid_back_recv, top_back_recv, out_recv,
    in_send, mid_send, top_send, mid_back_send, top_back_send, out_send, entered,
):
    ctx_count, mid_count, group, heads, own_rows, width = dims
    tok = own_rows * group
    mid_n, top_n = tok // MIDDLE_DILATION, tok // UPPER_DILATION
    ctx, me = lax.axis_index("ctx"), lax.axis_index("head")
    mid_base = ctx // mid_count * mid_count
    mid_me = ctx % mid_count
    sources = (query, key, value, out_grad)
    results = (attended_out, query_out, key_out, value_out)
    scale = width ** -0.5

    def signal_ctx(sem, low, high):
        def body(other, carry):
            pl.semaphore_signal(sem, inc=1, device_id={"ctx": other}, device_id_type=MESH)
            return carry

        lax.fori_loop(low, high, body, 0)

    barrier = pltpu.get_barrier_semaphore()
    for step in range(1, group):
        pl.semaphore_signal(barrier, inc=1, device_id={"head": (me + step) % group}, device_id_type=MESH)
    signal_ctx(barrier, ctx + 1, ctx_count)
    pl.semaphore_wait(barrier, group - 1 + ctx)

    wide = BUNDLE * width

    def columns(device, bundle):
        return pl.ds(pl.multiple_of(device * heads * width + bundle * wide, wide), wide)

    def lanes(head):
        return pl.ds(pl.multiple_of(head % BUNDLE * width, width), width)

    def rows_of(device):
        return pl.ds(pl.multiple_of(device * own_rows, own_rows), own_rows)

    def send_in(bundle, carry):
        for step in range(group):
            device = (me + step) % group
            for a in (1, 2, 0, 3):
                src = sources[a].at[:, columns(device, bundle)]
                dst = arrived.at[bundle, a, rows_of(me)]
                if step == 0:
                    pltpu.make_async_copy(src, dst, in_recv.at[bundle]).start()
                else:
                    pltpu.make_async_remote_copy(
                        src, dst, in_send.at[a], in_recv.at[bundle],
                        device_id={"head": device}, device_id_type=MESH,
                    ).start()
        return carry

    lax.fori_loop(0, heads // BUNDLE, send_in, 0)
    signal_ctx(entered, 0, ctx)

    @pl.when(ctx < ctx_count - 1)
    def _():
        pl.semaphore_wait(entered, ctx_count - 1 - ctx)

    def ring(count, place, base, src_of, dst, send_sem, recv_sem):
        def body(step, carry):
            other = (place + step) % count
            pltpu.make_async_remote_copy(
                src_of(other), dst, send_sem, recv_sem,
                device_id={"ctx": base + other}, device_id_type=MESH,
            ).start()
            return carry

        lax.fori_loop(1, count, body, 0)

    def wait_for(ref, sem):
        pltpu.make_async_copy(ref, ref, sem).wait()

    def gather_rows(head):
        bundle = head // BUNDLE

        @pl.when(head % BUNDLE == 0)
        def _():
            wait_for(arrived.at[bundle], in_recv.at[bundle])

        pick = one_hot((mid_n + top_n, tok), 0, tok, offsets[0, head], offsets[1, head], 1)
        key_rows = contract(pick, arrived[bundle, 1, :, lanes(head)], 1, 0)
        value_rows = contract(pick, arrived[bundle, 2, :, lanes(head)], 1, 0)
        mid = jnp.concatenate([key_rows[:mid_n], value_rows[:mid_n]], 0).astype(BF16)
        top = jnp.concatenate([key_rows[mid_n:], value_rows[mid_n:]], 0).astype(BF16)
        mid_own[head] = mid
        top_own[head] = top
        mid_rows_in[head, mid_me] = mid
        top_rows_in[head, ctx] = top
        ring(ctx_count, ctx, 0, lambda other: top_own.at[head], top_rows_in.at[head, ctx],
             top_send, top_recv.at[head])
        ring(mid_count, mid_me, mid_base, lambda other: mid_own.at[head], mid_rows_in.at[head, mid_me],
             mid_send, mid_recv.at[head])

    def hand_in(head, a, rows):
        bundle = head // BUNDLE
        staged[bundle, a, :, lanes(head)] = rows.astype(BF16)

        @pl.when(head % BUNDLE == BUNDLE - 1)
        def _():
            for step in range(group):
                device = (me + step) % group
                src = staged.at[bundle, a, rows_of(device)]
                dst = results[a].at[:, columns(me, bundle)]
                if step == 0:
                    pltpu.make_async_copy(src, dst, out_recv.at[a]).start()
                else:
                    pltpu.make_async_remote_copy(
                        src, dst, out_send.at[a], out_recv.at[a],
                        device_id={"head": device}, device_id_type=MESH,
                    ).start()

    def attend(head):
        wait_for(mid_rows_in.at[head, pl.ds(0, mid_count - 1)], mid_recv.at[head])
        wait_for(top_rows_in.at[head, pl.ds(0, ctx_count - 1)], top_recv.at[head])
        mid_in = mid_rows_in[head].astype(F32)
        top_in = top_rows_in[head].astype(F32)
        mid_all, top_all = mid_count * mid_n, ctx_count * top_n
        bundle = head // BUNDLE
        q, do = arrived[bundle, 0, :, lanes(head)], arrived[bundle, 3, :, lanes(head)]
        k = jnp.concatenate([
            arrived[bundle, 1, :, lanes(head)],
            mid_in[:, :mid_n].reshape(mid_all, width).astype(BF16),
            top_in[:, :top_n].reshape(top_all, width).astype(BF16),
        ], 0)
        v = jnp.concatenate([
            arrived[bundle, 2, :, lanes(head)],
            mid_in[:, mid_n:].reshape(mid_all, width).astype(BF16),
            top_in[:, top_n:].reshape(top_all, width).astype(BF16),
        ], 0)
        position = lax.broadcasted_iota(jnp.int32, (1, tok), 1)
        in_mid = position % MIDDLE_DILATION == offsets[0, head]
        in_top = position % UPPER_DILATION == offsets[1, head]
        score = contract(k, q, 1, 1) * (scale * math.log2(math.e))
        score = jnp.concatenate([
            score[:tok],
            jnp.where(in_mid, score[tok:tok + mid_all], LOWEST),
            jnp.where(in_top, score[tok + mid_all:], LOWEST),
        ], 0)
        top = jnp.max(score, 0, keepdims=True)
        weight = jnp.exp2(score - top)
        inverse = 1.0 / jnp.sum(weight, 0, keepdims=True)
        attended = (contract(v, weight.astype(BF16), 0, 0) * inverse).astype(BF16).astype(F32)
        delta = jnp.sum(do.astype(F32).T * attended, 0, keepdims=True)
        prob = weight * inverse
        dscore = (prob * (contract(v, do, 1, 1) - delta)).astype(BF16)
        hand_in(head, 0, attended.T)
        hand_in(head, 1, (contract(k, dscore, 0, 0) * scale).T)
        dk = contract(dscore, q, 1, 0) * scale
        dv = contract(prob.astype(BF16), do, 1, 0)
        partial[head % 2, 0] = dk[:tok]
        partial[head % 2, 1] = dv[:tok]

        def both(low, count, n):
            return jnp.concatenate([
                dk[low:low + count * n].reshape(count, n, width),
                dv[low:low + count * n].reshape(count, n, width),
            ], 1).astype(BF16)

        mid_back[head] = both(tok, mid_count, mid_n)
        top_back[head] = both(tok + mid_all, ctx_count, top_n)
        ring(ctx_count, ctx, 0, lambda other: top_back.at[head, other], top_back_in.at[head, ctx],
             top_back_send, top_back_recv.at[head])
        ring(mid_count, mid_me, mid_base, lambda other: mid_back.at[head, other], mid_back_in.at[head, mid_me],
             mid_back_send, mid_back_recv.at[head])
        top_back_in[head, ctx] = top_back[head, ctx]
        mid_back_in[head, mid_me] = mid_back[head, mid_me]

    def finish(head):
        wait_for(mid_back_in.at[head, pl.ds(0, mid_count - 1)], mid_back_recv.at[head])
        wait_for(top_back_in.at[head, pl.ds(0, ctx_count - 1)], top_back_recv.at[head])
        mid = jnp.sum(mid_back_in[head].astype(F32), 0)
        top = jnp.sum(top_back_in[head].astype(F32), 0)
        rows = jnp.concatenate([
            jnp.concatenate([mid[:mid_n], top[:top_n]], 0),
            jnp.concatenate([mid[mid_n:], top[top_n:]], 0),
        ], 1)
        high = rows.astype(BF16).astype(F32)
        both = jnp.concatenate([high, rows - high], 0).astype(BF16)
        place = one_hot((tok, 2 * (mid_n + top_n)), 1, tok, offsets[0, head], offsets[1, head], 2)
        added = contract(place, both, 1, 0)
        hand_in(head, 2, partial[head % 2, 0] + added[:, :width])
        hand_in(head, 3, partial[head % 2, 1] + added[:, width:])

    gather_rows(0)

    def turn(head, carry):
        @pl.when(head < heads - 1)
        def _():
            gather_rows(head + 1)

        attend(head)

        @pl.when(head > 0)
        def _():
            finish(head - 1)

        return carry

    lax.fori_loop(0, heads, turn, 0)
    finish(heads - 1)

    others = pl.ds(0, own_rows * (group - 1))
    for a in range(4):
        wait_for(results[a], out_recv.at[a])
        wait_for(staged.at[:, a, others], out_send.at[a])
        wait_for(arrived.at[:, a, others], in_send.at[a])
    wait_for(mid_rows_in.at[:, pl.ds(0, mid_count - 1)], mid_send)
    wait_for(top_rows_in.at[:, pl.ds(0, ctx_count - 1)], top_send)
    wait_for(mid_back_in.at[:, pl.ds(0, mid_count - 1)], mid_back_send)
    wait_for(top_back_in.at[:, pl.ds(0, ctx_count - 1)], top_back_send)


def hand_over(*refs):
    sources, results, sem = refs[:4], refs[4:8], refs[8]
    copies = [pltpu.make_async_copy(src, dst, sem.at[i]) for i, (src, dst) in enumerate(zip(sources, results))]
    for copy in copies:
        copy.start()
    for copy in copies:
        copy.wait()


def local(query, key, value, out_grad, offsets):
    ctx_count, group = lax.axis_size("ctx"), lax.axis_size("head")
    heads = offsets.shape[1]
    own_rows = query.shape[0]
    width = query.shape[1] // (group * heads)
    tok = own_rows * group
    mid_count = ctx_count // MIDDLE_SEGMENTS
    mid_n, top_n = tok // MIDDLE_DILATION, tok // UPPER_DILATION
    dims = (ctx_count, mid_count, group, heads, own_rows, width)
    anywhere = pl.BlockSpec(memory_space=pl.ANY)
    dma = pltpu.SemaphoreType.DMA
    landed = pl.pallas_call(
        functools.partial(kernel, dims),
        out_shape=tuple(pltpu.VMEM(query.shape, BF16) for _ in range(4)),
        in_specs=[pl.BlockSpec(memory_space=pltpu.SMEM)] + [anywhere] * 4,
        out_specs=(anywhere,) * 4,
        scratch_shapes=[
            pltpu.VMEM((heads // BUNDLE, 4, tok, BUNDLE * width), BF16),
            pltpu.VMEM((heads // BUNDLE, 4, tok, BUNDLE * width), BF16),
            pltpu.VMEM((2, 2, tok, width), F32),
            pltpu.VMEM((heads, 2 * mid_n, width), BF16),
            pltpu.VMEM((heads, mid_count, 2 * mid_n, width), BF16),
            pltpu.VMEM((heads, 2 * top_n, width), BF16),
            pltpu.VMEM((heads, ctx_count, 2 * top_n, width), BF16),
            pltpu.VMEM((heads, mid_count, 2 * mid_n, width), BF16),
            pltpu.VMEM((heads, mid_count, 2 * mid_n, width), BF16),
            pltpu.VMEM((heads, ctx_count, 2 * top_n, width), BF16),
            pltpu.VMEM((heads, ctx_count, 2 * top_n, width), BF16),
            dma((heads,)), dma((heads,)), dma((heads,)), dma((heads,)), dma((heads,)), dma((4,)),
            dma((4,)), dma, dma, dma, dma, dma((4,)), pltpu.SemaphoreType.REGULAR,
        ],
        compiler_params=pltpu.CompilerParams(
            collective_id=0, has_side_effects=True, vmem_limit_bytes=59 * 1024 * 1024
        ),
        cost_estimate=pl.CostEstimate(
            flops=12 * heads * tok * (tok + 128) * width,
            bytes_accessed=16 * query.size,
            transcendentals=heads * tok * (tok + 128),
        ),
        name="dilated_attention",
    )(offsets, query, key, value, out_grad)
    return pl.pallas_call(
        hand_over,
        out_shape=tuple(jax.ShapeDtypeStruct(query.shape, BF16) for _ in range(4)),
        in_specs=[anywhere] * 4,
        out_specs=(anywhere,) * 4,
        scratch_shapes=[dma((4,))],
        compiler_params=pltpu.CompilerParams(vmem_limit_bytes=16 * 1024 * 1024),
        name="hand_over",
    )(*(pltpu.with_memory_space_constraint(x, pltpu.VMEM) for x in landed))


def solution(mesh):
    rows = P(("ctx", "head"), None)
    return jax.shard_map(
        local, mesh=mesh, in_specs=(rows,) * 4 + (P(None, "head"),), out_specs=(rows,) * 4, check_vma=False
    )
```

```python
import functools
import math

import jax
import jax.numpy as jnp
from jax import lax
from jax.experimental import pallas as pl
from jax.experimental.pallas import tpu as pltpu
from jax.sharding import PartitionSpec as P

MIDDLE_DILATION = 16
UPPER_DILATION = 64
MIDDLE_SEGMENTS = 4
LOWEST = -1e30
BUNDLE = 2
CORES = 2
HAND_OVER_CUTS = 4
MESH = pl.DeviceIdType.MESH
F32 = jnp.float32
BF16 = jnp.bfloat16


def contract(a, b, dim_a, dim_b):
    return lax.dot_general(a, b, (((dim_a,), (dim_b,)), ((), ())), preferred_element_type=F32)


def one_hot(shape, row_dim, tok, middle_offset, upper_offset, copies):
    mid_rows, top_rows = tok // MIDDLE_DILATION, tok // UPPER_DILATION
    rows = lax.broadcasted_iota(jnp.int32, shape, row_dim)
    token = lax.broadcasted_iota(jnp.int32, shape, 1 - row_dim)
    if copies > 1:
        rows = jnp.where(rows >= mid_rows + top_rows, rows - (mid_rows + top_rows), rows)
    owner = jnp.where(
        rows < mid_rows,
        rows * MIDDLE_DILATION + middle_offset,
        (rows - mid_rows) * UPPER_DILATION + upper_offset,
    )
    return jnp.where(token == owner, 1.0, 0.0).astype(BF16)


def kernel(
    dims,
    offsets, query, key, value, out_grad,
    attended_out, query_out, key_out, value_out,
    arrived, staged, partial,
    mid_own, mid_rows_in, top_own, top_rows_in,
    mid_back, mid_back_in, top_back, top_back_in,
    in_recv, mid_recv, top_recv, mid_back_recv, top_back_recv, out_recv,
    in_send, mid_send, top_send, mid_back_send, top_back_send, out_send, entered,
):
    ctx_count, mid_count, group, heads, own_rows, width = dims
    tok = own_rows * group
    mid_n, top_n = tok // MIDDLE_DILATION, tok // UPPER_DILATION
    ctx, me = lax.axis_index("ctx"), lax.axis_index("head")
    mid_base = ctx // mid_count * mid_count
    mid_me = ctx % mid_count
    sources = (query, key, value, out_grad)
    results = (attended_out, query_out, key_out, value_out)
    scale = width ** -0.5
    chips = group // CORES
    partners = [
        (me // CORES + chip) % chips * CORES + (me + core) % CORES
        for chip in range(1, chips) for core in range(CORES)
    ] + [me // CORES * CORES + (me + core) % CORES for core in range(1, CORES)] + [me]

    def signal_ctx(sem, low, high):
        def body(other, carry):
            pl.semaphore_signal(sem, inc=1, device_id={"ctx": other}, device_id_type=MESH)
            return carry

        lax.fori_loop(low, high, body, 0)

    barrier = pltpu.get_barrier_semaphore()
    for step in range(1, group):
        pl.semaphore_signal(barrier, inc=1, device_id={"head": (me + step) % group}, device_id_type=MESH)
    signal_ctx(barrier, ctx + 1, ctx_count)
    pl.semaphore_wait(barrier, group - 1 + ctx)

    wide = BUNDLE * width

    def columns(device, bundle):
        return pl.ds(pl.multiple_of(device * heads * width + bundle * wide, wide), wide)

    def lanes(head):
        return pl.ds(pl.multiple_of(head % BUNDLE * width, width), width)

    def rows_of(device):
        return pl.ds(pl.multiple_of(device * own_rows, own_rows), own_rows)

    def send_in(bundle, carry):
        for device in partners:
            for a in (1, 2, 0, 3):
                src = sources[a].at[:, columns(device, bundle)]
                dst = arrived.at[bundle, a, rows_of(me)]
                if device is me:
                    pltpu.make_async_copy(src, dst, in_recv.at[bundle]).start()
                else:
                    pltpu.make_async_remote_copy(
                        src, dst, in_send.at[a], in_recv.at[bundle],
                        device_id={"head": device}, device_id_type=MESH,
                    ).start()
        return carry

    lax.fori_loop(0, heads // BUNDLE, send_in, 0)
    signal_ctx(entered, 0, ctx)

    @pl.when(ctx < ctx_count - 1)
    def _():
        pl.semaphore_wait(entered, ctx_count - 1 - ctx)

    def ring(count, place, base, src_of, dst, send_sem, recv_sem):
        def body(step, carry):
            other = (place + step) % count
            pltpu.make_async_remote_copy(
                src_of(other), dst, send_sem, recv_sem,
                device_id={"ctx": base + other}, device_id_type=MESH,
            ).start()
            return carry

        lax.fori_loop(1, count, body, 0)

    def wait_for(ref, sem):
        pltpu.make_async_copy(ref, ref, sem).wait()

    def gather_rows(head):
        bundle = head // BUNDLE

        @pl.when(head % BUNDLE == 0)
        def _():
            wait_for(arrived.at[bundle], in_recv.at[bundle])

        pick = one_hot((mid_n + top_n, tok), 0, tok, offsets[0, head], offsets[1, head], 1)
        key_rows = contract(pick, arrived[bundle, 1, :, lanes(head)], 1, 0)
        value_rows = contract(pick, arrived[bundle, 2, :, lanes(head)], 1, 0)
        mid = jnp.concatenate([key_rows[:mid_n], value_rows[:mid_n]], 0).astype(BF16)
        top = jnp.concatenate([key_rows[mid_n:], value_rows[mid_n:]], 0).astype(BF16)
        mid_own[head] = mid
        top_own[head] = top
        mid_rows_in[head, mid_me] = mid
        top_rows_in[head, ctx] = top
        ring(ctx_count, ctx, 0, lambda other: top_own.at[head], top_rows_in.at[head, ctx],
             top_send, top_recv.at[head])
        ring(mid_count, mid_me, mid_base, lambda other: mid_own.at[head], mid_rows_in.at[head, mid_me],
             mid_send, mid_recv.at[head])

    def hand_in(head, a, rows):
        bundle = head // BUNDLE
        staged[bundle, a, :, lanes(head)] = rows.astype(BF16)

        @pl.when(head % BUNDLE == BUNDLE - 1)
        def _():
            for device in partners:
                src = staged.at[bundle, a, rows_of(device)]
                dst = results[a].at[:, columns(me, bundle)]
                if device is me:
                    pltpu.make_async_copy(src, dst, out_recv.at[a]).start()
                else:
                    pltpu.make_async_remote_copy(
                        src, dst, out_send.at[a], out_recv.at[a],
                        device_id={"head": device}, device_id_type=MESH,
                    ).start()

    def attend(head):
        wait_for(mid_rows_in.at[head, pl.ds(0, mid_count - 1)], mid_recv.at[head])
        wait_for(top_rows_in.at[head, pl.ds(0, ctx_count - 1)], top_recv.at[head])
        mid_in = mid_rows_in[head].astype(F32)
        top_in = top_rows_in[head].astype(F32)
        mid_all, top_all = mid_count * mid_n, ctx_count * top_n
        bundle = head // BUNDLE
        q, do = arrived[bundle, 0, :, lanes(head)], arrived[bundle, 3, :, lanes(head)]
        k = jnp.concatenate([
            arrived[bundle, 1, :, lanes(head)],
            mid_in[:, :mid_n].reshape(mid_all, width).astype(BF16),
            top_in[:, :top_n].reshape(top_all, width).astype(BF16),
        ], 0)
        v = jnp.concatenate([
            arrived[bundle, 2, :, lanes(head)],
            mid_in[:, mid_n:].reshape(mid_all, width).astype(BF16),
            top_in[:, top_n:].reshape(top_all, width).astype(BF16),
        ], 0)
        position = lax.broadcasted_iota(jnp.int32, (1, tok), 1)
        in_mid = position % MIDDLE_DILATION == offsets[0, head]
        in_top = position % UPPER_DILATION == offsets[1, head]
        score = contract(k, q, 1, 1) * (scale * math.log2(math.e))
        score = jnp.concatenate([
            score[:tok],
            jnp.where(in_mid, score[tok:tok + mid_all], LOWEST),
            jnp.where(in_top, score[tok + mid_all:], LOWEST),
        ], 0)
        top = jnp.max(score, 0, keepdims=True)
        weight = jnp.exp2(score - top)
        inverse = 1.0 / jnp.sum(weight, 0, keepdims=True)
        attended = (contract(v, weight.astype(BF16), 0, 0) * inverse).astype(BF16).astype(F32)
        delta = jnp.sum(do.astype(F32).T * attended, 0, keepdims=True)
        prob = weight * inverse
        dscore = (prob * (contract(v, do, 1, 1) - delta)).astype(BF16)
        hand_in(head, 0, attended.T)
        hand_in(head, 1, (contract(k, dscore, 0, 0) * scale).T)
        dk = contract(dscore, q, 1, 0) * scale
        dv = contract(prob.astype(BF16), do, 1, 0)
        partial[head % 2, 0] = dk[:tok]
        partial[head % 2, 1] = dv[:tok]

        def both(low, count, n):
            return jnp.concatenate([
                dk[low:low + count * n].reshape(count, n, width),
                dv[low:low + count * n].reshape(count, n, width),
            ], 1).astype(BF16)

        mid_back[head] = both(tok, mid_count, mid_n)
        top_back[head] = both(tok + mid_all, ctx_count, top_n)
        ring(ctx_count, ctx, 0, lambda other: top_back.at[head, other], top_back_in.at[head, ctx],
             top_back_send, top_back_recv.at[head])
        ring(mid_count, mid_me, mid_base, lambda other: mid_back.at[head, other], mid_back_in.at[head, mid_me],
             mid_back_send, mid_back_recv.at[head])
        top_back_in[head, ctx] = top_back[head, ctx]
        mid_back_in[head, mid_me] = mid_back[head, mid_me]

    def finish(head):
        wait_for(mid_back_in.at[head, pl.ds(0, mid_count - 1)], mid_back_recv.at[head])
        wait_for(top_back_in.at[head, pl.ds(0, ctx_count - 1)], top_back_recv.at[head])
        mid = jnp.sum(mid_back_in[head].astype(F32), 0)
        top = jnp.sum(top_back_in[head].astype(F32), 0)
        rows = jnp.concatenate([
            jnp.concatenate([mid[:mid_n], top[:top_n]], 0),
            jnp.concatenate([mid[mid_n:], top[top_n:]], 0),
        ], 1)
        high = rows.astype(BF16).astype(F32)
        both = jnp.concatenate([high, rows - high], 0).astype(BF16)
        place = one_hot((tok, 2 * (mid_n + top_n)), 1, tok, offsets[0, head], offsets[1, head], 2)
        added = contract(place, both, 1, 0)
        hand_in(head, 2, partial[head % 2, 0] + added[:, :width])
        hand_in(head, 3, partial[head % 2, 1] + added[:, width:])

    def turn(head, carry):
        @pl.when(head < heads)
        def _():
            gather_rows(head)

        @pl.when((head >= 1) & (head <= heads))
        def _():
            attend(head - 1)

        @pl.when(head >= 2)
        def _():
            finish(head - 2)

        return carry

    lax.fori_loop(0, heads + 2, turn, 0)

    others = pl.ds(0, own_rows * (group - 1))
    for a in range(4):
        wait_for(results[a], out_recv.at[a])
        wait_for(staged.at[:, a, others], out_send.at[a])
        wait_for(arrived.at[:, a, others], in_send.at[a])
    wait_for(mid_rows_in.at[:, pl.ds(0, mid_count - 1)], mid_send)
    wait_for(top_rows_in.at[:, pl.ds(0, ctx_count - 1)], top_send)
    wait_for(mid_back_in.at[:, pl.ds(0, mid_count - 1)], mid_back_send)
    wait_for(top_back_in.at[:, pl.ds(0, ctx_count - 1)], top_back_send)


def hand_over(*refs):
    sources, results, sems = refs[:4], refs[4:8], refs[8]
    rows = sources[0].shape[0] // HAND_OVER_CUTS
    copies = [
        pltpu.make_async_copy(src.at[pl.ds(cut * rows, rows)], dst.at[pl.ds(cut * rows, rows)], sems.at[i, cut])
        for i, (src, dst) in enumerate(zip(sources, results)) for cut in range(HAND_OVER_CUTS)
    ]
    for copy in copies:
        copy.start()
    for copy in copies:
        copy.wait()


def local(query, key, value, out_grad, offsets):
    ctx_count, group = lax.axis_size("ctx"), lax.axis_size("head")
    heads = offsets.shape[1]
    own_rows = query.shape[0]
    width = query.shape[1] // (group * heads)
    tok = own_rows * group
    mid_count = ctx_count // MIDDLE_SEGMENTS
    mid_n, top_n = tok // MIDDLE_DILATION, tok // UPPER_DILATION
    dims = (ctx_count, mid_count, group, heads, own_rows, width)
    anywhere = pl.BlockSpec(memory_space=pl.ANY)
    dma = pltpu.SemaphoreType.DMA
    landed = pl.pallas_call(
        functools.partial(kernel, dims),
        out_shape=tuple(pltpu.VMEM(query.shape, BF16) for _ in range(4)),
        in_specs=[pl.BlockSpec(memory_space=pltpu.SMEM)] + [anywhere] * 4,
        out_specs=(anywhere,) * 4,
        scratch_shapes=[
            pltpu.VMEM((heads // BUNDLE, 4, tok, BUNDLE * width), BF16),
            pltpu.VMEM((heads // BUNDLE, 4, tok, BUNDLE * width), BF16),
            pltpu.VMEM((2, 2, tok, width), F32),
            pltpu.VMEM((heads, 2 * mid_n, width), BF16),
            pltpu.VMEM((heads, mid_count, 2 * mid_n, width), BF16),
            pltpu.VMEM((heads, 2 * top_n, width), BF16),
            pltpu.VMEM((heads, ctx_count, 2 * top_n, width), BF16),
            pltpu.VMEM((heads, mid_count, 2 * mid_n, width), BF16),
            pltpu.VMEM((heads, mid_count, 2 * mid_n, width), BF16),
            pltpu.VMEM((heads, ctx_count, 2 * top_n, width), BF16),
            pltpu.VMEM((heads, ctx_count, 2 * top_n, width), BF16),
            dma((heads,)), dma((heads,)), dma((heads,)), dma((heads,)), dma((heads,)), dma((4,)),
            dma((4,)), dma, dma, dma, dma, dma((4,)), pltpu.SemaphoreType.REGULAR,
        ],
        compiler_params=pltpu.CompilerParams(
            collective_id=0, has_side_effects=True, vmem_limit_bytes=59 * 1024 * 1024
        ),
        cost_estimate=pl.CostEstimate(
            flops=12 * heads * tok * (tok + 128) * width,
            bytes_accessed=16 * query.size,
            transcendentals=heads * tok * (tok + 128),
        ),
        name="dilated_attention",
    )(offsets, query, key, value, out_grad)
    return pl.pallas_call(
        hand_over,
        out_shape=tuple(jax.ShapeDtypeStruct(query.shape, BF16) for _ in range(4)),
        in_specs=[anywhere] * 4,
        out_specs=(anywhere,) * 4,
        scratch_shapes=[dma((4, HAND_OVER_CUTS))],
        compiler_params=pltpu.CompilerParams(vmem_limit_bytes=16 * 1024 * 1024),
        name="hand_over",
    )(*(pltpu.with_memory_space_constraint(x, pltpu.VMEM) for x in landed))


def solution(mesh):
    rows = P(("ctx", "head"), None)
    return jax.shard_map(
        local, mesh=mesh, in_specs=(rows,) * 4 + (P(None, "head"),), out_specs=(rows,) * 4, check_vma=False
    )
```

```python
import functools
import math

import jax
import jax.numpy as jnp
from jax import lax
from jax.experimental import pallas as pl
from jax.experimental.pallas import tpu as pltpu
from jax.sharding import PartitionSpec as P

MIDDLE_DILATION = 16
UPPER_DILATION = 64
MIDDLE_SEGMENTS = 4
LOWEST = -1e30
BUNDLE = 2
CORES = 2
HAND_OVER_CUTS = 2
MESH = pl.DeviceIdType.MESH
F32 = jnp.float32
BF16 = jnp.bfloat16


def contract(a, b, dim_a, dim_b):
    return lax.dot_general(a, b, (((dim_a,), (dim_b,)), ((), ())), preferred_element_type=F32)


def one_hot(shape, row_dim, tok, middle_offset, upper_offset, copies):
    mid_rows, top_rows = tok // MIDDLE_DILATION, tok // UPPER_DILATION
    rows = lax.broadcasted_iota(jnp.int32, shape, row_dim)
    token = lax.broadcasted_iota(jnp.int32, shape, 1 - row_dim)
    if copies > 1:
        rows = jnp.where(rows >= mid_rows + top_rows, rows - (mid_rows + top_rows), rows)
    owner = jnp.where(
        rows < mid_rows,
        rows * MIDDLE_DILATION + middle_offset,
        (rows - mid_rows) * UPPER_DILATION + upper_offset,
    )
    return jnp.where(token == owner, 1.0, 0.0).astype(BF16)


def kernel(
    dims,
    offsets, query, key, value, out_grad,
    attended_out, query_out, key_out, value_out,
    arrived, staged, partial,
    mid_own, mid_rows_in, top_own, top_rows_in,
    mid_back, mid_back_in, top_back, top_back_in,
    in_recv, mid_recv, top_recv, mid_back_recv, top_back_recv, out_recv,
    in_send, mid_send, top_send, mid_back_send, top_back_send, out_send, entered,
):
    ctx_count, mid_count, group, heads, own_rows, width = dims
    tok = own_rows * group
    mid_n, top_n = tok // MIDDLE_DILATION, tok // UPPER_DILATION
    ctx, me = lax.axis_index("ctx"), lax.axis_index("head")
    mid_base = ctx // mid_count * mid_count
    mid_me = ctx % mid_count
    sources = (query, key, value, out_grad)
    results = (attended_out, query_out, key_out, value_out)
    scale = width ** -0.5
    chips = group // CORES
    partners = [
        (me // CORES + chip) % chips * CORES + (me + core) % CORES
        for chip in range(1, chips) for core in range(CORES)
    ] + [me // CORES * CORES + (me + core) % CORES for core in range(1, CORES)] + [me]

    def signal_ctx(sem, low, high):
        def body(other, carry):
            pl.semaphore_signal(sem, inc=1, device_id={"ctx": other}, device_id_type=MESH)
            return carry

        lax.fori_loop(low, high, body, 0)

    barrier = pltpu.get_barrier_semaphore()
    for step in range(1, group):
        pl.semaphore_signal(barrier, inc=1, device_id={"head": (me + step) % group}, device_id_type=MESH)
    signal_ctx(barrier, ctx + 1, ctx_count)
    pl.semaphore_wait(barrier, group - 1 + ctx)

    wide = BUNDLE * width

    def columns(device, bundle):
        return pl.ds(pl.multiple_of(device * heads * width + bundle * wide, wide), wide)

    def lanes(head):
        return pl.ds(pl.multiple_of(head % BUNDLE * width, width), width)

    def rows_of(device):
        return pl.ds(pl.multiple_of(device * own_rows, own_rows), own_rows)

    def send_in(bundle, carry):
        for device in partners:
            for a in (1, 2, 0, 3):
                src = sources[a].at[:, columns(device, bundle)]
                dst = arrived.at[bundle, a, rows_of(me)]
                if device is me:
                    pltpu.make_async_copy(src, dst, in_recv.at[bundle]).start()
                else:
                    pltpu.make_async_remote_copy(
                        src, dst, in_send.at[a], in_recv.at[bundle],
                        device_id={"head": device}, device_id_type=MESH,
                    ).start()
        return carry

    lax.fori_loop(0, heads // BUNDLE, send_in, 0)
    signal_ctx(entered, 0, ctx)

    @pl.when(ctx < ctx_count - 1)
    def _():
        pl.semaphore_wait(entered, ctx_count - 1 - ctx)

    def ring(count, place, base, src_of, dst, send_sem, recv_sem):
        def body(step, carry):
            other = (place + step) % count
            pltpu.make_async_remote_copy(
                src_of(other), dst, send_sem, recv_sem,
                device_id={"ctx": base + other}, device_id_type=MESH,
            ).start()
            return carry

        lax.fori_loop(1, count, body, 0)

    def wait_for(ref, sem):
        pltpu.make_async_copy(ref, ref, sem).wait()

    def gather_rows(head):
        bundle = head // BUNDLE

        @pl.when(head % BUNDLE == 0)
        def _():
            wait_for(arrived.at[bundle], in_recv.at[bundle])

        pick = one_hot((mid_n + top_n, tok), 0, tok, offsets[0, head], offsets[1, head], 1)
        key_rows = contract(pick, arrived[bundle, 1, :, lanes(head)], 1, 0)
        value_rows = contract(pick, arrived[bundle, 2, :, lanes(head)], 1, 0)
        mid = jnp.concatenate([key_rows[:mid_n], value_rows[:mid_n]], 0).astype(BF16)
        top = jnp.concatenate([key_rows[mid_n:], value_rows[mid_n:]], 0).astype(BF16)
        mid_own[head] = mid
        top_own[head] = top
        mid_rows_in[head, mid_me] = mid
        top_rows_in[head, ctx] = top
        ring(ctx_count, ctx, 0, lambda other: top_own.at[head], top_rows_in.at[head, ctx],
             top_send, top_recv.at[head])
        ring(mid_count, mid_me, mid_base, lambda other: mid_own.at[head], mid_rows_in.at[head, mid_me],
             mid_send, mid_recv.at[head])

    def hand_in(head, a, rows):
        bundle = head // BUNDLE
        staged[bundle, a, :, lanes(head)] = rows.astype(BF16)

        @pl.when(head % BUNDLE == BUNDLE - 1)
        def _():
            for device in partners:
                src = staged.at[bundle, a, rows_of(device)]
                dst = results[a].at[:, columns(me, bundle)]
                if device is me:
                    pltpu.make_async_copy(src, dst, out_recv.at[a]).start()
                else:
                    pltpu.make_async_remote_copy(
                        src, dst, out_send.at[a], out_recv.at[a],
                        device_id={"head": device}, device_id_type=MESH,
                    ).start()

    def attend(head):
        wait_for(mid_rows_in.at[head, pl.ds(0, mid_count - 1)], mid_recv.at[head])
        wait_for(top_rows_in.at[head, pl.ds(0, ctx_count - 1)], top_recv.at[head])
        mid_in = mid_rows_in[head].astype(F32)
        top_in = top_rows_in[head].astype(F32)
        mid_all, top_all = mid_count * mid_n, ctx_count * top_n
        bundle = head // BUNDLE
        q, do = arrived[bundle, 0, :, lanes(head)], arrived[bundle, 3, :, lanes(head)]
        k = jnp.concatenate([
            arrived[bundle, 1, :, lanes(head)],
            mid_in[:, :mid_n].reshape(mid_all, width).astype(BF16),
            top_in[:, :top_n].reshape(top_all, width).astype(BF16),
        ], 0)
        v = jnp.concatenate([
            arrived[bundle, 2, :, lanes(head)],
            mid_in[:, mid_n:].reshape(mid_all, width).astype(BF16),
            top_in[:, top_n:].reshape(top_all, width).astype(BF16),
        ], 0)
        position = lax.broadcasted_iota(jnp.int32, (1, tok), 1)
        in_mid = position % MIDDLE_DILATION == offsets[0, head]
        in_top = position % UPPER_DILATION == offsets[1, head]
        score = contract(k, q, 1, 1) * (scale * math.log2(math.e))
        score = jnp.concatenate([
            score[:tok],
            jnp.where(in_mid, score[tok:tok + mid_all], LOWEST),
            jnp.where(in_top, score[tok + mid_all:], LOWEST),
        ], 0)
        top = jnp.max(score, 0, keepdims=True)
        weight = jnp.exp2(score - top)
        inverse = 1.0 / jnp.sum(weight, 0, keepdims=True)
        attended = (contract(v, weight.astype(BF16), 0, 0) * inverse).astype(BF16).astype(F32)
        delta = jnp.sum(do.astype(F32).T * attended, 0, keepdims=True)
        prob = weight * inverse
        dscore = (prob * (contract(v, do, 1, 1) - delta)).astype(BF16)
        hand_in(head, 0, attended.T)
        hand_in(head, 1, (contract(k, dscore, 0, 0) * scale).T)
        dk = contract(dscore, q, 1, 0) * scale
        dv = contract(prob.astype(BF16), do, 1, 0)
        partial[head % 2, 0] = dk[:tok]
        partial[head % 2, 1] = dv[:tok]

        def both(low, count, n):
            return jnp.concatenate([
                dk[low:low + count * n].reshape(count, n, width),
                dv[low:low + count * n].reshape(count, n, width),
            ], 1).astype(BF16)

        mid_back[head] = both(tok, mid_count, mid_n)
        top_back[head] = both(tok + mid_all, ctx_count, top_n)
        ring(ctx_count, ctx, 0, lambda other: top_back.at[head, other], top_back_in.at[head, ctx],
             top_back_send, top_back_recv.at[head])
        ring(mid_count, mid_me, mid_base, lambda other: mid_back.at[head, other], mid_back_in.at[head, mid_me],
             mid_back_send, mid_back_recv.at[head])
        top_back_in[head, ctx] = top_back[head, ctx]
        mid_back_in[head, mid_me] = mid_back[head, mid_me]

    def finish(head):
        wait_for(mid_back_in.at[head, pl.ds(0, mid_count - 1)], mid_back_recv.at[head])
        wait_for(top_back_in.at[head, pl.ds(0, ctx_count - 1)], top_back_recv.at[head])
        mid = jnp.sum(mid_back_in[head].astype(F32), 0)
        top = jnp.sum(top_back_in[head].astype(F32), 0)
        rows = jnp.concatenate([
            jnp.concatenate([mid[:mid_n], top[:top_n]], 0),
            jnp.concatenate([mid[mid_n:], top[top_n:]], 0),
        ], 1)
        high = rows.astype(BF16).astype(F32)
        both = jnp.concatenate([high, rows - high], 0).astype(BF16)
        place = one_hot((tok, 2 * (mid_n + top_n)), 1, tok, offsets[0, head], offsets[1, head], 2)
        added = contract(place, both, 1, 0)
        hand_in(head, 2, partial[head % 2, 0] + added[:, :width])
        hand_in(head, 3, partial[head % 2, 1] + added[:, width:])

    gather_rows(0)

    def turn(head, carry):
        @pl.when(head < heads - 1)
        def _():
            gather_rows(head + 1)

        attend(head)

        @pl.when(head > 0)
        def _():
            finish(head - 1)

        return carry

    lax.fori_loop(0, heads, turn, 0)
    finish(heads - 1)

    others = pl.ds(0, own_rows * (group - 1))
    for a in range(4):
        wait_for(results[a], out_recv.at[a])
        wait_for(staged.at[:, a, others], out_send.at[a])
        wait_for(arrived.at[:, a, others], in_send.at[a])
    wait_for(mid_rows_in.at[:, pl.ds(0, mid_count - 1)], mid_send)
    wait_for(top_rows_in.at[:, pl.ds(0, ctx_count - 1)], top_send)
    wait_for(mid_back_in.at[:, pl.ds(0, mid_count - 1)], mid_back_send)
    wait_for(top_back_in.at[:, pl.ds(0, ctx_count - 1)], top_back_send)


def hand_over(*refs):
    sources, results, sems = refs[:4], refs[4:8], refs[8]
    rows = sources[0].shape[0] // HAND_OVER_CUTS
    copies = [
        pltpu.make_async_copy(src.at[pl.ds(cut * rows, rows)], dst.at[pl.ds(cut * rows, rows)], sems.at[i, cut])
        for i, (src, dst) in enumerate(zip(sources, results)) for cut in range(HAND_OVER_CUTS)
    ]
    for i, copy in enumerate(copies):
        copy.start(priority=i % 2)
    for copy in copies:
        copy.wait()


def local(query, key, value, out_grad, offsets):
    ctx_count, group = lax.axis_size("ctx"), lax.axis_size("head")
    heads = offsets.shape[1]
    own_rows = query.shape[0]
    width = query.shape[1] // (group * heads)
    tok = own_rows * group
    mid_count = ctx_count // MIDDLE_SEGMENTS
    mid_n, top_n = tok // MIDDLE_DILATION, tok // UPPER_DILATION
    dims = (ctx_count, mid_count, group, heads, own_rows, width)
    anywhere = pl.BlockSpec(memory_space=pl.ANY)
    dma = pltpu.SemaphoreType.DMA
    landed = pl.pallas_call(
        functools.partial(kernel, dims),
        out_shape=tuple(pltpu.VMEM(query.shape, BF16) for _ in range(4)),
        in_specs=[pl.BlockSpec(memory_space=pltpu.SMEM)] + [anywhere] * 4,
        out_specs=(anywhere,) * 4,
        scratch_shapes=[
            pltpu.VMEM((heads // BUNDLE, 4, tok, BUNDLE * width), BF16),
            pltpu.VMEM((heads // BUNDLE, 4, tok, BUNDLE * width), BF16),
            pltpu.VMEM((2, 2, tok, width), F32),
            pltpu.VMEM((heads, 2 * mid_n, width), BF16),
            pltpu.VMEM((heads, mid_count, 2 * mid_n, width), BF16),
            pltpu.VMEM((heads, 2 * top_n, width), BF16),
            pltpu.VMEM((heads, ctx_count, 2 * top_n, width), BF16),
            pltpu.VMEM((heads, mid_count, 2 * mid_n, width), BF16),
            pltpu.VMEM((heads, mid_count, 2 * mid_n, width), BF16),
            pltpu.VMEM((heads, ctx_count, 2 * top_n, width), BF16),
            pltpu.VMEM((heads, ctx_count, 2 * top_n, width), BF16),
            dma((heads,)), dma((heads,)), dma((heads,)), dma((heads,)), dma((heads,)), dma((4,)),
            dma((4,)), dma, dma, dma, dma, dma((4,)), pltpu.SemaphoreType.REGULAR,
        ],
        compiler_params=pltpu.CompilerParams(
            collective_id=0, has_side_effects=True, vmem_limit_bytes=59 * 1024 * 1024
        ),
        cost_estimate=pl.CostEstimate(
            flops=12 * heads * tok * (tok + 128) * width,
            bytes_accessed=16 * query.size,
            transcendentals=heads * tok * (tok + 128),
        ),
        name="dilated_attention",
    )(offsets, query, key, value, out_grad)
    return pl.pallas_call(
        hand_over,
        out_shape=tuple(jax.ShapeDtypeStruct(query.shape, BF16) for _ in range(4)),
        in_specs=[anywhere] * 4,
        out_specs=(anywhere,) * 4,
        scratch_shapes=[dma((4, HAND_OVER_CUTS))],
        compiler_params=pltpu.CompilerParams(vmem_limit_bytes=16 * 1024 * 1024),
        name="hand_over",
    )(*(pltpu.with_memory_space_constraint(x, pltpu.VMEM) for x in landed))


def solution(mesh):
    rows = P(("ctx", "head"), None)
    return jax.shard_map(
        local, mesh=mesh, in_specs=(rows,) * 4 + (P(None, "head"),), out_specs=(rows,) * 4, check_vma=False
    )
```
